32 devices in a mesh: major: 4 (over y, x), minor: 8 (over z, core).
Axes of the slice: x: 2, y: 2, z: 4, core: 2. Of those that a mesh axis runs over, the one named last changes fastest.
Arguments:
- block_in: bfloat16 [4096, 1024], P(('major', 'minor')), may hold values from -6 to 6
- out_cot: bfloat16 [4096, 1024], P(('major', 'minor')), may hold values from -6 to 6
- w_in: bfloat16 [1024, 3072], replicated, may hold values from -0.1875 to 0.1875
- w_out: bfloat16 [1024, 1024], replicated, may hold values from -0.1875 to 0.1875
- conv_one: bfloat16 [4096, 1024], P(('major', 'minor')), may hold values from -6 to 6
- conv_two: bfloat16 [4096, 1024], P(('major', 'minor')), may hold values from -6 to 6
- filter_one: bfloat16 [4096, 1024], P(('major', 'minor')), may hold values from -6 to 6
- filter_two: bfloat16 [4096, 1024], P(('major', 'minor')), may hold values from -6 to 6
Outputs:
- in_grad: bfloat16 [4096, 1024], P(('major', 'minor'))
- w_in_grad: float32 [1024, 3072], P(('major', 'minor'))
- w_out_grad: float32 [1024, 1024], P(('major', 'minor'))
- filter_one_grad: bfloat16 [4096, 1024], P(('major', 'minor'))
- filter_two_grad: bfloat16 [4096, 1024], P(('major', 'minor'))
The draws below stay inside these ranges and needn't reach their ends.
All inputs are finite; a program needn't handle non-finite values.
Results may differ from the reference program's by a relative error of at most 0.014.
Values may be sent and summed in bfloat16 or wider, within the bound.
No kernel may reach another device: no remote copies, remote signals or barrier semaphores. Data moves between devices by JAX's collectives and lax.ppermute only.
A program may use at most 128 MiB of HBM per device.

```python
import jax
import jax.numpy as jnp

D = 1024
TOKENS = 4096


def with_spikes(array, rng, source, target, parts, factor):
    owner, partner = [(jnp.arange(array.shape[dim]) // (array.shape[dim] // parts)).reshape([-1 if axis == dim else 1 for axis in range(array.ndim)]) for dim in (source, target)]
    chosen = jax.random.permutation(rng, parts)[partner]
    strong = (owner == chosen) | (owner == (partner + parts // 2) % parts)
    return jnp.where(strong, factor * array, array)


def steps_of(key, shape, cuts, low, top_value):
    level = 1.0
    for dim, shards_of in cuts:
        steps = jax.random.uniform(jax.random.fold_in(jax.random.fold_in(key, 6), dim), (shards_of,), jnp.float32, low / len(cuts), top_value / len(cuts))
        level = level * jnp.repeat(jnp.exp(steps), shape[dim] // shards_of).reshape((-1,) + (1,) * (len(shape) - 1 - dim))
    return level


def centred(key, dims, deviation, most, shards=(), kind=jnp.bfloat16):
    entries = jax.random.normal(key, dims, jnp.float32) * deviation
    if len(shards) > 0:
        entries = steps_of(key, dims, shards, -0.22, 0.18) * entries
    return jnp.clip(entries, min=-most, max=most).astype(kind)


def bell_draw_with(own_key, dims, width, reach, split, heavy, kind=jnp.bfloat16):
    result = width * jax.random.normal(own_key, dims, jnp.float32)
    if split:
        result = result * steps_of(own_key, dims, split, -0.22, 0.18)
    return jnp.clip(with_spikes(result, jax.random.fold_in(own_key, 3), *heavy), -reach, reach).astype(kind)


def setup_inputs(seed: int = 0) -> dict:
    key_list = jax.random.split(jax.random.key(seed), 9)
    block_in = bell_draw_with(key_list[0], (TOKENS, D), 1.0, 6.0, ((0, 32),), (0, 1, 32, 2.75))
    out_cot = centred(key_list[1], (TOKENS, D), 1.0, 6.0, ((0, 32),))
    w_in = centred(key_list[2], (D, 3 * D), D ** -0.5, 0.1875)
    w_out = centred(key_list[3], (D, D), D ** -0.5, 0.1875)
    conv_one = centred(key_list[4], (TOKENS, D), 1.0, 6.0, ((0, 32),))
    conv_two = centred(key_list[5], (TOKENS, D), 1.0, 6.0, ((0, 32),))
    filter_one = centred(key_list[6], (TOKENS, D), 1.0, 6.0, ((0, 32),))
    filter_two = centred(key_list[7], (TOKENS, D), 1.0, 6.0, ((0, 32),))
    return {"block_in": block_in, "out_cot": out_cot, "w_in": w_in, "w_out": w_out, "conv_one": conv_one, "conv_two": conv_two, "filter_one": filter_one, "filter_two": filter_two}


def spectrum(field):
    return jnp.fft.rfft(field.astype(jnp.float32), n=2 * TOKENS, axis=0)


def correlate(left_spec, right_spec):
    return jnp.fft.irfft(left_spec * jnp.conj(right_spec), n=2 * TOKENS, axis=0)[:TOKENS]


def product(left, right):
    return (left.astype(jnp.float32) * right.astype(jnp.float32)).astype(jnp.bfloat16)


def reference(block_in, out_cot, w_in, w_out, conv_one, conv_two, filter_one, filter_two):
    scale = TOKENS ** -0.5
    proj = jnp.dot(block_in, w_in, preferred_element_type=jnp.float32).astype(jnp.bfloat16)
    value = proj[:, :D]
    gate_one = proj[:, D:2 * D]
    gate_two = proj[:, 2 * D:]
    first_out = product(gate_one, conv_one)
    second_out = product(gate_two, conv_two)
    grad_second = jnp.dot(out_cot, w_out.T, preferred_element_type=jnp.float32).astype(jnp.bfloat16)
    grad_conv_two = product(grad_second, gate_two)
    grad_gate_two = product(grad_second, conv_two)
    spec_two = spectrum(grad_conv_two)
    grad_first = (correlate(spec_two, spectrum(filter_two)) * scale).astype(jnp.bfloat16)
    filter_two_grad = (correlate(spec_two, spectrum(first_out)) * scale).astype(jnp.bfloat16)
    grad_conv_one = product(grad_first, gate_one)
    grad_gate_one = product(grad_first, conv_one)
    spec_one = spectrum(grad_conv_one)
    grad_value = (correlate(spec_one, spectrum(filter_one)) * scale).astype(jnp.bfloat16)
    filter_one_grad = (correlate(spec_one, spectrum(value)) * scale).astype(jnp.bfloat16)
    grad_proj = jnp.concatenate([grad_value, grad_gate_one, grad_gate_two], axis=1)
    in_grad = jnp.dot(grad_proj, w_in.T, preferred_element_type=jnp.float32).astype(jnp.bfloat16)
    w_in_grad = jnp.dot(block_in.T, grad_proj, preferred_element_type=jnp.float32) * scale
    w_out_grad = jnp.dot(second_out.T, out_cot, preferred_element_type=jnp.float32) * scale
    return in_grad, w_in_grad, w_out_grad, filter_one_grad, filter_two_grad
```

```python
import functools
import math

import jax
import jax.numpy as jnp
import numpy as np
from jax import lax
from jax.experimental import pallas as pl
from jax.experimental.pallas import tpu as pltpu
from jax.sharding import PartitionSpec as P

AXES = ("major", "minor")
LAST = (((1,), (1,)), ((), ()))


def product(left, right):
    return (left.astype(jnp.float32) * right.astype(jnp.float32)).astype(jnp.bfloat16)


def tables(devices, rows_dev):
    seq_len = devices * rows_dev
    line = np.arange(rows_dev)
    angle = -2.0 * math.pi * (line[:, None] * line[None, :] % rows_dev) / rows_dev
    cos, sin = np.cos(angle), np.sin(angle)
    forward = np.block([[cos, sin], [-sin, cos]])
    backward = np.block([[cos, -sin], [sin, cos]])
    turn = -2.0 * math.pi * (np.arange(devices)[:, None] + 0.25) * line[None, :] / seq_len
    turn_cos = np.repeat(np.cos(turn), 8, axis=0)
    turn_sin = np.repeat(np.sin(turn), 8, axis=0)
    return (
        jnp.asarray(forward, jnp.bfloat16),
        jnp.asarray(backward, jnp.bfloat16),
        jnp.asarray(turn_cos, jnp.float32),
        jnp.asarray(turn_sin, jnp.float32),
    )


def fft_real(xs):
    size = len(xs)
    if size == 1:
        return [(xs[0], None)]
    if size == 2:
        turned = xs[1] * math.cos(math.pi / 4)
        return [(xs[0] + turned, -turned), (xs[0] - turned, turned)]
    even, odd = fft_real(xs[0::2]), fft_real(xs[1::2])
    low, high = [], []
    for k in range(size // 2):
        angle = -2.0 * math.pi * (k + 0.25) / size
        cos, sin = math.cos(angle), math.sin(angle)
        (er, ei), (orr, oi) = even[k], odd[k]
        tr = orr * cos - oi * sin
        ti = orr * sin + oi * cos
        low.append((er + tr, ei + ti))
        high.append((er - tr, ei - ti))
    return low + high


def fft_back(pairs):
    size = len(pairs)
    if size == 2:
        (ar, ai), (br, bi) = pairs
        return [ar + br, ((ar - br) - (ai - bi)) * math.cos(math.pi / 4)]
    half = size // 2
    even, odd = [], []
    for k in range(half):
        angle = 2.0 * math.pi * (k + 0.25) / size
        cos, sin = math.cos(angle), math.sin(angle)
        (ar, ai), (br, bi) = pairs[k], pairs[k + half]
        even.append((ar + br, ai + bi))
        dr, di = ar - br, ai - bi
        odd.append((dr * cos - di * sin, dr * sin + di * cos))
    even, odd = fft_back(even), fft_back(odd)
    return [term for pair in zip(even, odd) for term in pair]


def long_kernel(
    devices, group, scale,
    grad_two, filter_two, gate_one, conv_one, filter_one, value, forward, backward, turn_cos, turn_sin,
    gate_grad, filter_two_grad, value_grad, filter_one_grad,
    held, grad_one, spec_a, spec_b, spec_c,
):
    rows = devices * group
    cols = held.shape[1]
    halves = group // 8

    def into(source, spec):
        if source is not held:
            held[...] = source[...].astype(jnp.float32)

        def step(j, carry):
            xs = [held[pl.ds(n * group + j * 8, 8), :] for n in range(devices)]
            for k, (re, im) in enumerate(fft_real(xs)):
                cos, sin = turn_cos[8 * k : 8 * k + 8, :], turn_sin[8 * k : 8 * k + 8, :]
                at = pl.ds(k * group + j * 8, 8)
                spec[at, :cols] = re * cos - im * sin
                spec[at, cols:] = re * sin + im * cos
            return carry

        lax.fori_loop(0, halves, step, 0)

    def outof(spec):
        def step(j, carry):
            pairs = []
            for k in range(devices):
                cos, sin = turn_cos[8 * k : 8 * k + 8, :], turn_sin[8 * k : 8 * k + 8, :]
                at = pl.ds(k * group + j * 8, 8)
                re, im = spec[at, :cols], spec[at, cols:]
                pairs.append((re * cos + im * sin, im * cos - re * sin))
            for n, term in enumerate(fft_back(pairs)):
                held[pl.ds(n * group + j * 8, 8), :] = term * scale
            return carry

        lax.fori_loop(0, halves, step, 0)

    def correlate():
        block = min(rows, 256)

        def step(i, carry):
            at = pl.ds(pl.multiple_of(i * block, block), block)

            def line(spec):
                moved = jnp.dot(spec[at, :].astype(jnp.bfloat16), forward[...], preferred_element_type=jnp.float32)
                return moved[:, :cols], moved[:, cols:]

            ar, ai = line(spec_a)
            for spec in (spec_b, spec_c):
                br, bi = line(spec)
                mixed = jnp.concatenate([ar * br + ai * bi, ai * br - ar * bi], axis=1).astype(jnp.bfloat16)
                spec[at, :] = jnp.dot(mixed, backward[...], preferred_element_type=jnp.float32)
            return carry

        lax.fori_loop(0, rows // block, step, 0)

    into(grad_two, spec_a)
    into(filter_two, spec_b)
    held[...] = product(gate_one[...], conv_one[...]).astype(jnp.float32)
    into(held, spec_c)
    correlate()
    outof(spec_c)
    filter_two_grad[...] = held[...].astype(jnp.bfloat16)
    outof(spec_b)
    grad_first = held[...].astype(jnp.bfloat16)
    gate_grad[...] = product(grad_first, conv_one[...])
    held[...] = product(grad_first, gate_one[...]).astype(jnp.float32)
    into(held, spec_a)
    into(filter_one, spec_b)
    into(value, spec_c)
    correlate()
    outof(spec_b)
    value_grad[...] = held[...].astype(jnp.bfloat16)
    outof(spec_c)
    filter_one_grad[...] = held[...].astype(jnp.bfloat16)


def long_convs(fields, devices, group, rows_dev):
    rows = devices * group
    seq_len = devices * rows_dev
    scale = seq_len ** (-0.5) / seq_len
    field = jax.ShapeDtypeStruct((rows, rows_dev), jnp.bfloat16)
    spec = pltpu.VMEM((rows, 2 * rows_dev), jnp.float32)
    return pl.pallas_call(
        functools.partial(long_kernel, devices, group, scale),
        out_shape=[field] * 4,
        in_specs=[pl.BlockSpec(memory_space=pltpu.VMEM)] * 10,
        out_specs=[pl.BlockSpec(memory_space=pltpu.VMEM)] * 4,
        scratch_shapes=[pltpu.VMEM((rows, rows_dev), jnp.float32), pltpu.VMEM((8, rows_dev), jnp.float32), spec, spec, spec],
        compiler_params=pltpu.CompilerParams(vmem_limit_bytes=40 * 2**20),
    )(*fields, *tables(devices, rows_dev))


def pair_gather(block, axis):
    count = lax.axis_size(axis)
    held, step = block[None], 1
    while step < count:
        other = lax.ppermute(held, axis, [(i, i ^ step) for i in range(count)])
        high = (lax.axis_index(axis) & step) != 0
        held = jnp.concatenate([jnp.where(high, other, held), jnp.where(high, held, other)])
        step *= 2
    return held


def shards(block_in, out_cot, w_in, w_out, conv_one, conv_two, filter_one, filter_two):
    rows_dev, width = block_in.shape
    devices, majors, minors = lax.axis_size(AXES), lax.axis_size("major"), lax.axis_size("minor")
    group = width // devices
    scale = (rows_dev * devices) ** (-0.5)
    all_in = lax.all_gather(block_in, AXES, axis=0, tiled=False)
    major_cot = pair_gather(out_cot, "major")
    first = (((0,), (1,)), ((), ()))
    proj = lax.dot_general(w_in, block_in, first, preferred_element_type=jnp.float32).astype(jnp.bfloat16)
    value, gate_one, gate_two = proj[:width], proj[width : 2 * width], proj[2 * width :]
    grad_second = lax.dot_general(w_out, out_cot, LAST, preferred_element_type=jnp.float32).astype(jnp.bfloat16)
    conv_two = conv_two.T
    second_out = product(gate_two, conv_two)
    grad_conv_two = product(grad_second, gate_two)
    grad_gate_two = product(grad_second, conv_two)
    moving = jnp.concatenate(
        [grad_conv_two, filter_two.T, gate_one, conv_one.T, filter_one.T, value, grad_gate_two]
    )
    moving = lax.optimization_barrier(moving).reshape(7, devices, group, rows_dev)
    here = lax.all_to_all(moving, AXES, split_axis=1, concat_axis=1, tiled=True)
    fields = [here[i].reshape(devices * group, rows_dev) for i in range(6)]
    major_out = lax.all_to_all(
        second_out.reshape(majors, width // majors, rows_dev), "major", split_axis=0, concat_axis=0, tiled=True
    )
    out_part = jnp.einsum("mct,mtw->cw", major_out, major_cot, preferred_element_type=jnp.float32)
    out_part = out_part.astype(jnp.bfloat16).reshape(minors, group, width)
    out_part = lax.all_to_all(out_part, "minor", split_axis=0, concat_axis=0, tiled=True)
    w_out_grad = out_part.astype(jnp.float32).sum(axis=0) * scale
    gate_grad, filter_two_grad, value_grad, filter_one_grad = long_convs(fields, devices, group, rows_dev)
    by_device = lambda x: x.reshape(devices, group, rows_dev)
    grads = jnp.stack([by_device(value_grad), by_device(gate_grad), here[6]])
    in_part = jnp.einsum("dtw,fdct->wfc", all_in, grads, preferred_element_type=jnp.float32) * scale
    in_part = in_part.astype(jnp.bfloat16).reshape(devices, group, 3 * group)
    in_part = lax.all_to_all(in_part, AXES, split_axis=0, concat_axis=0, tiled=True)
    w_in_grad = in_part.reshape(devices, group, 3, group).transpose(1, 2, 0, 3).reshape(group, 3 * width)
    back = jnp.concatenate([value_grad, gate_grad, filter_one_grad, filter_two_grad])
    back = lax.optimization_barrier(back).reshape(4, devices, group, rows_dev)
    back = lax.all_to_all(back, AXES, split_axis=1, concat_axis=1, tiled=True).reshape(4, width, rows_dev)
    grad_proj = jnp.concatenate([back[0], back[1], grad_gate_two], axis=0)
    in_grad = lax.dot_general(grad_proj, w_in, (((0,), (1,)), ((), ())), preferred_element_type=jnp.float32)
    return in_grad.astype(jnp.bfloat16), w_in_grad.astype(jnp.float32), w_out_grad, back[2].T, back[3].T


def solution(mesh):
    tokens = P(AXES, None)
    return jax.shard_map(
        shards,
        mesh=mesh,
        in_specs=(tokens, tokens, P(), P(), tokens, tokens, tokens, tokens),
        out_specs=(tokens,) * 5,
        check_vma=False,
    )
```

```python
import functools
import math

import jax
import jax.numpy as jnp
import numpy as np
from jax import lax
from jax.experimental import pallas as pl
from jax.experimental.pallas import tpu as pltpu
from jax.sharding import PartitionSpec as P

AXES = ("major", "minor")
LAST = (((1,), (1,)), ((), ()))


def product(left, right):
    return (left.astype(jnp.float32) * right.astype(jnp.float32)).astype(jnp.bfloat16)


def tables(devices, rows_dev):
    seq_len = devices * rows_dev
    line = np.arange(rows_dev)
    angle = -2.0 * math.pi * (line[:, None] * line[None, :] % rows_dev) / rows_dev
    cos, sin = np.cos(angle), np.sin(angle)
    forward = np.block([[cos, sin], [-sin, cos]])
    backward = np.block([[cos, -sin], [sin, cos]])
    turn = -2.0 * math.pi * (np.arange(devices)[:, None] + 0.25) * line[None, :] / seq_len
    turn_cos = np.repeat(np.cos(turn), 8, axis=0)
    turn_sin = np.repeat(np.sin(turn), 8, axis=0)
    return (
        jnp.asarray(forward, jnp.bfloat16),
        jnp.asarray(backward, jnp.bfloat16),
        jnp.asarray(turn_cos, jnp.float32),
        jnp.asarray(turn_sin, jnp.float32),
    )


def fft_real(xs):
    size = len(xs)
    if size == 1:
        return [(xs[0], None)]
    if size == 2:
        turned = xs[1] * math.cos(math.pi / 4)
        return [(xs[0] + turned, -turned), (xs[0] - turned, turned)]
    even, odd = fft_real(xs[0::2]), fft_real(xs[1::2])
    low, high = [], []
    for k in range(size // 2):
        angle = -2.0 * math.pi * (k + 0.25) / size
        cos, sin = math.cos(angle), math.sin(angle)
        (er, ei), (orr, oi) = even[k], odd[k]
        tr = orr * cos - oi * sin
        ti = orr * sin + oi * cos
        low.append((er + tr, ei + ti))
        high.append((er - tr, ei - ti))
    return low + high


def fft_back(pairs):
    size = len(pairs)
    if size == 2:
        (ar, ai), (br, bi) = pairs
        return [ar + br, ((ar - br) - (ai - bi)) * math.cos(math.pi / 4)]
    half = size // 2
    even, odd = [], []
    for k in range(half):
        angle = 2.0 * math.pi * (k + 0.25) / size
        cos, sin = math.cos(angle), math.sin(angle)
        (ar, ai), (br, bi) = pairs[k], pairs[k + half]
        even.append((ar + br, ai + bi))
        dr, di = ar - br, ai - bi
        odd.append((dr * cos - di * sin, dr * sin + di * cos))
    even, odd = fft_back(even), fft_back(odd)
    return [term for pair in zip(even, odd) for term in pair]


def transforms(devices, group, held, turn_cos, turn_sin):
    cols = held.shape[1]

    def into(spec):
        def step(j, carry):
            xs = [held[pl.ds(n * group + j * 8, 8), :] for n in range(devices)]
            for k, (re, im) in enumerate(fft_real(xs)):
                cos, sin = turn_cos[8 * k : 8 * k + 8, :], turn_sin[8 * k : 8 * k + 8, :]
                at = pl.ds(k * group + j * 8, 8)
                spec[at, :cols] = re * cos - im * sin
                spec[at, cols:] = re * sin + im * cos
            return carry

        lax.fori_loop(0, group // 8, step, 0)

    def outof(spec, scale):
        def step(j, carry):
            pairs = []
            for k in range(devices):
                cos, sin = turn_cos[8 * k : 8 * k + 8, :], turn_sin[8 * k : 8 * k + 8, :]
                at = pl.ds(k * group + j * 8, 8)
                re, im = spec[at, :cols], spec[at, cols:]
                pairs.append((re * cos + im * sin, im * cos - re * sin))
            for n, term in enumerate(fft_back(pairs)):
                held[pl.ds(n * group + j * 8, 8), :] = term * scale
            return carry

        lax.fori_loop(0, group // 8, step, 0)

    return into, outof


def correlate(spec_a, spec_b, spec_c, forward, backward):
    rows, cols = spec_a.shape[0], spec_a.shape[1] // 2
    block = min(rows, 256)

    def step(i, carry):
        at = pl.ds(pl.multiple_of(i * block, block), block)

        def line(spec):
            moved = jnp.dot(spec[at, :].astype(jnp.bfloat16), forward[...], preferred_element_type=jnp.float32)
            return moved[:, :cols], moved[:, cols:]

        ar, ai = line(spec_a)
        for spec in (spec_b, spec_c):
            br, bi = line(spec)
            mixed = jnp.concatenate([ar * br + ai * bi, ai * br - ar * bi], axis=1).astype(jnp.bfloat16)
            spec[at, :] = jnp.dot(mixed, backward[...], preferred_element_type=jnp.float32)
        return carry

    lax.fori_loop(0, rows // block, step, 0)


def fetch(sources, slots, done):
    copies = [pltpu.make_async_copy(source, slot, done.at[i]) for i, (source, slot) in enumerate(zip(sources, slots))]
    for copy in copies:
        copy.start()
    return copies


def begin_kernel(
    square, conv_one, filter_two, filter_one, out_cot, conv_two, block_in, w_out, w_in,
    sent, second_out, late, rows_here, w_out_here, w_in_here, done,
):
    devices, _, group, lanes = sent.shape
    width = out_cot.shape[1]
    copies = fetch(
        [conv_one, filter_two, filter_one, out_cot, w_out, conv_two, block_in] + [w_in.at[:, i * width : (i + 1) * width] for i in (2, 1, 0)],
        [rows_here.at[i] for i in range(4)] + [w_out_here, rows_here.at[4], rows_here.at[5]] + [w_in_here.at[i] for i in (2, 1, 0)],
        done,
    )

    def turned(x):
        parts = [
            lax.dot_general(square[...], x[:, at : at + lanes], LAST, preferred_element_type=jnp.float32)
            for at in range(0, width, lanes)
        ]
        return jnp.concatenate(parts, axis=0).astype(jnp.bfloat16)

    def send(i, x):
        sent[:, i] = turned(x).reshape(devices, group, lanes)

    def project(i):
        return jnp.dot(rows_here[5], w_in_here[i], preferred_element_type=jnp.float32).astype(jnp.bfloat16)

    for i in range(3):
        copies[i].wait()
        send(i, rows_here[i])
    copies[3].wait()
    copies[4].wait()
    grad_second = lax.dot_general(rows_here[3], w_out_here[...], LAST, preferred_element_type=jnp.float32).astype(jnp.bfloat16)
    copies[5].wait()
    grad_gate_two = product(grad_second, rows_here[4])
    late[...] = grad_gate_two
    send(6, grad_gate_two)
    copies[6].wait()
    copies[7].wait()
    gate_two = project(2)
    send(3, product(grad_second, gate_two))
    second_out[...] = turned(product(gate_two, rows_here[4]))
    copies[8].wait()
    send(4, project(1))
    copies[9].wait()
    send(5, project(0))


def middle_kernel(scale, me, here, forward, backward, turn_cos, turn_sin, back, slab, held, spec_a, spec_b, spec_c):
    devices, _, group, cols = here.shape
    rows = devices * group
    into, outof = transforms(devices, group, held, turn_cos, turn_sin)
    flat = lambda i: here[:, i].astype(jnp.float32).reshape(rows, cols)
    blocks = lambda x: x.astype(jnp.bfloat16).reshape(devices, group, cols)

    def lay(kind, x):
        for n in range(devices):
            place = n ^ me[0]
            at = pl.ds(pl.multiple_of(((place & 1) * (devices // 2) + (place >> 1)) * cols, cols), cols)
            slab[kind * group : (kind + 1) * group, at] = x[n * group : (n + 1) * group].astype(slab.dtype)

    held[...] = flat(3)
    into(spec_a)
    held[...] = flat(1)
    into(spec_b)
    held[...] = (flat(4) * flat(0)).astype(jnp.bfloat16).astype(jnp.float32)
    into(spec_c)
    correlate(spec_a, spec_b, spec_c, forward, backward)
    outof(spec_c, scale)
    back[:, 3] = blocks(held[...])
    outof(spec_b, scale)
    grad_first = held[...].astype(jnp.bfloat16).astype(jnp.float32)
    gate_grad = grad_first * flat(0)
    back[:, 1] = blocks(gate_grad)
    lay(1, gate_grad)
    held[...] = (grad_first * flat(4)).astype(jnp.bfloat16).astype(jnp.float32)
    into(spec_a)
    held[...] = flat(2)
    into(spec_b)
    held[...] = flat(5)
    into(spec_c)
    lay(2, flat(6))
    slab[3 * group :, :] = jnp.zeros((cols - 3 * group, devices * cols), slab.dtype)
    correlate(spec_a, spec_b, spec_c, forward, backward)
    outof(spec_c, scale)
    back[:, 2] = blocks(held[...])
    outof(spec_b, scale)
    back[:, 0] = blocks(held[...])
    lay(0, held[...])


def slab_kernel(scale, slab, *refs):
    *pieces, part, slots, done = refs
    count, (depth, steps, width) = len(pieces), slots.shape
    devices, group, cols = part.shape
    copies = [pltpu.make_async_copy(piece, slots.at[i % depth], done.at[i]) for i, piece in enumerate(pieces)]
    for copy in copies[:depth]:
        copy.start()
    total = jnp.zeros((cols, width), jnp.float32)
    for i, copy in enumerate(copies):
        copy.wait()
        total += jnp.dot(slab[:, i * steps : (i + 1) * steps], slots[i % depth], preferred_element_type=jnp.float32)
        if i + depth < count:
            copies[i + depth].start()
    part[...] = (total * scale).T.astype(jnp.bfloat16).reshape(devices, group, cols)


def on_chip(kernel, out_shape, args, scratch=(), far=(), vmem_mib=48):
    vmem = pl.BlockSpec(memory_space=pltpu.VMEM)
    spaces = [pltpu.SMEM if x.dtype == jnp.int32 else pltpu.HBM if i in far else pltpu.VMEM for i, x in enumerate(args)]
    return pl.pallas_call(
        kernel,
        out_shape=out_shape,
        in_specs=[pl.BlockSpec(memory_space=space) for space in spaces],
        out_specs=jax.tree.map(lambda _: vmem, out_shape),
        scratch_shapes=list(scratch),
        compiler_params=pltpu.CompilerParams(vmem_limit_bytes=vmem_mib * 2**20),
    )(*args)


def long_convs(rows, rows_dev):
    spec = pltpu.VMEM((rows, 2 * rows_dev), jnp.float32)
    return [pltpu.VMEM((rows, rows_dev), jnp.float32), spec, spec, spec]


def home_kernel(square, home, part, w_in, in_grad, filter_one_grad, filter_two_grad, home_here, part_here, w_in_here, done):
    devices, _, group, lanes = home.shape
    width = devices * group
    copies = fetch(
        [home, part] + [w_in.at[:, i * width : (i + 1) * width] for i in range(2)],
        [home_here, part_here] + [w_in_here.at[i] for i in range(2)],
        done,
    )

    def whole(i):
        field = home_here[:, i].astype(jnp.float32).reshape(width, lanes).astype(jnp.bfloat16)
        return lax.dot_general(square[...], field, LAST, preferred_element_type=jnp.float32).astype(jnp.bfloat16)

    copies[0].wait()
    filter_one_grad[...] = whole(2)
    filter_two_grad[...] = whole(3)
    copies[1].wait()
    total = part_here[...]
    for i in (0, 1):
        copies[2 + i].wait()
        total += lax.dot_general(whole(i), w_in_here[i], LAST, preferred_element_type=jnp.float32)
    in_grad[...] = total.astype(jnp.bfloat16)


def place_kernel(taken, moves, w_in_grad):
    devices, group, lanes = taken.shape
    per, kinds = moves.shape[0], moves.shape[2] // lanes
    for g in range(devices // per):
        total = jnp.zeros((group, kinds * lanes), jnp.float32)
        for s in range(per):
            total += jnp.dot(taken[g * per + s], moves[s], preferred_element_type=jnp.float32)
        for f in range(kinds):
            at = f * devices * group + g * lanes
            w_in_grad[:, at : at + lanes] = total[:, f * lanes : (f + 1) * lanes]


def moves_of(group, lanes, kinds):
    per = lanes // group
    table = np.zeros((per, lanes, kinds * lanes), np.float32)
    for s in range(per):
        for f in range(kinds):
            for c in range(group):
                table[s, f * group + c, f * lanes + s * group + c] = 1.0
    return jnp.asarray(table, jnp.bfloat16)


def bits_of(count):
    return [1 << i for i in range(count.bit_length() - 1)]


def swap(block, axis, bit):
    return lax.ppermute(block, axis, [(i, i ^ bit) for i in range(lax.axis_size(axis))])


def after(x, *others):
    return lax.optimization_barrier((x, *others))[0]


def near_chips(block):
    bits = bits_of(lax.axis_size("minor"))[1:]
    blocks = [block] + [None] * (2 ** len(bits) - 1)
    for bit in bits:
        blocks[bit // 2] = swap(block, "minor", bit)
    return blocks


def far_chips(blocks, later):
    blocks = [block if block is None else after(block, later) for block in blocks]
    for j in range(1, len(blocks)):
        low = j & -j
        if j != low:
            blocks[j] = swap(blocks[j ^ low], "minor", 2 * low)
    return blocks


def major_near(blocks):
    half = max(len(blocks) // 2, 1)
    lines = []
    for part in (blocks[:half], blocks[half:]):
        held = [jnp.concatenate(part)] + [None] * (lax.axis_size("major") - 1)
        for bit in bits_of(lax.axis_size("major")):
            held[bit] = swap(held[0], "major", bit)
        lines.append(held)
    return lines


def gather_chips(lines, later):
    pieces = []
    for turn, line in enumerate(lines):
        held = [piece if piece is None else after(piece, later) for piece in line]
        for j in range(1, len(held)):
            bit = j & -j if turn else 1 << (j.bit_length() - 1)
            if j != bit:
                held[j] = swap(held[j ^ bit], "major", bit)
        pieces.append(held)
    return [piece for pair in zip(*pieces) for piece in pair]


def out_part(second_out, cots):
    width, rows_dev = second_out.shape
    majors, minors = lax.axis_size("major"), lax.axis_size("minor")
    mine = lax.axis_index("major")
    slabs = second_out.reshape(majors, width // majors, rows_dev)
    slab = [lax.dynamic_index_in_dim(slabs, mine ^ j, 0, keepdims=False) for j in range(majors)]
    slab = jnp.stack([swap(part, "major", j) if j else part for j, part in enumerate(slab)])
    total = jnp.einsum("mct,mtw->cw", slab, jnp.stack(cots), preferred_element_type=jnp.float32)
    total = total.reshape(minors // 2, 2, -1, total.shape[1])
    mine = lax.axis_index("minor") % 2
    part = lambda core: lax.dynamic_index_in_dim(total, core, 1, keepdims=False)
    return part(mine) + swap(part(1 - mine), "minor", 1)


def out_sum(total):
    mine = lax.axis_index("minor") // 2
    part = lambda chip: lax.dynamic_index_in_dim(total, chip, 0, keepdims=False)
    sums = part(mine)
    for j in range(1, total.shape[0]):
        sums += swap(part(mine ^ j).astype(jnp.bfloat16), "minor", 2 * j).astype(jnp.float32)
    return sums


def regroup(x):
    return lax.all_to_all(x, AXES, split_axis=0, concat_axis=0, tiled=True)


def shards(block_in, out_cot, w_in, w_out, conv_one, conv_two, filter_one, filter_two):
    rows_dev, width = block_in.shape
    devices, majors = lax.axis_size(AXES), lax.axis_size("major")
    group = width // devices
    scale = (rows_dev * devices) ** (-0.5)
    fft_scale = scale / (rows_dev * devices)
    field = lambda *dims: jax.ShapeDtypeStruct((devices, *dims, group, rows_dev), jnp.bfloat16)
    array = lambda *dims: jax.ShapeDtypeStruct(dims, jnp.bfloat16)

    near_in = near_chips(block_in)
    square = jnp.eye(rows_dev, dtype=jnp.bfloat16)
    sent, second_out, late = on_chip(
        begin_kernel,
        [field(7), array(width, rows_dev), array(rows_dev, width)],
        (square, conv_one, filter_two, filter_one, out_cot, conv_two, block_in, w_out, w_in),
        [
            pltpu.VMEM((6, rows_dev, width), jnp.bfloat16),
            pltpu.VMEM((width, width), jnp.bfloat16),
            pltpu.VMEM((3, width, width), jnp.bfloat16),
            pltpu.SemaphoreType.DMA((10,)),
        ],
        range(1, 9),
        60,
    )
    cots = [swap(out_cot, "major", j) if j else out_cot for j in range(majors)]
    sent = after(sent, *cots, *[block for block in near_in if block is not None])
    here = regroup(sent)
    total = out_part(after(second_out, sent), cots)
    late = lax.dot_general(late, w_in[:, 2 * width :], LAST, preferred_element_type=jnp.float32)
    lines = major_near(far_chips(near_in, sent))
    here = after(here, late, total, *[piece for line in lines for piece in line if piece is not None])

    spec = pltpu.VMEM((devices * group, 2 * rows_dev), jnp.float32)
    back, slab = on_chip(
        functools.partial(middle_kernel, fft_scale),
        [field(4), array(rows_dev, devices * rows_dev)],
        (lax.axis_index(AXES).astype(jnp.int32)[None], here, *tables(devices, rows_dev)),
        [pltpu.VMEM((devices * group, rows_dev), jnp.float32), spec, spec, spec],
    )
    home = regroup(back)
    all_in = gather_chips(lines, back)
    all_in += [swap(piece, "minor", 1) for piece in all_in]
    w_out_grad = out_sum(after(total, back)) * scale

    rows = all_in[0].shape[0]
    slots = min(len(all_in), 16 * 2**20 // (2 * rows * width))
    part = on_chip(
        functools.partial(slab_kernel, scale),
        field(),
        (slab, *all_in),
        [pltpu.VMEM((slots, rows, width), jnp.bfloat16), pltpu.SemaphoreType.DMA((len(all_in),))],
        range(1, 1 + len(all_in)),
        60,
    )
    taken = regroup(after(part, home, w_out_grad))
    in_grad, filter_one_grad, filter_two_grad = on_chip(
        home_kernel,
        [array(rows_dev, width)] * 3,
        (square, home, late, w_in),
        [
            pltpu.VMEM(home.shape, jnp.bfloat16),
            pltpu.VMEM((rows_dev, width), jnp.float32),
            pltpu.VMEM((2, width, width), jnp.bfloat16),
            pltpu.SemaphoreType.DMA((4,)),
        ],
        range(1, 4),
        60,
    )
    w_in_grad = on_chip(
        place_kernel, jax.ShapeDtypeStruct((group, 3 * width), jnp.float32), (taken, moves_of(group, rows_dev, 3))
    )
    return in_grad, w_in_grad, w_out_grad, filter_one_grad, filter_two_grad


def solution(mesh):
    tokens = P(AXES, None)
    return jax.shard_map(
        shards,
        mesh=mesh,
        in_specs=(tokens, tokens, P(), P(), tokens, tokens, tokens, tokens),
        out_specs=(tokens,) * 5,
        check_vma=False,
    )
```

```python
import functools
import math

import jax
import jax.numpy as jnp
import numpy as np
from jax import lax
from jax.experimental import pallas as pl
from jax.experimental.pallas import tpu as pltpu
from jax.sharding import PartitionSpec as P

AXES = ("major", "minor")
LAST = (((1,), (1,)), ((), ()))


def product(left, right):
    return (left.astype(jnp.float32) * right.astype(jnp.float32)).astype(jnp.bfloat16)


def tables(devices, rows_dev):
    seq_len = devices * rows_dev
    line = np.arange(rows_dev)
    angle = -2.0 * math.pi * (line[:, None] * line[None, :] % rows_dev) / rows_dev
    cos, sin = np.cos(angle), np.sin(angle)
    forward = np.block([[cos, sin], [-sin, cos]])
    backward = np.block([[cos, -sin], [sin, cos]])
    turn = -2.0 * math.pi * (np.arange(devices)[:, None] + 0.25) * line[None, :] / seq_len
    turn_cos = np.repeat(np.cos(turn), 8, axis=0)
    turn_sin = np.repeat(np.sin(turn), 8, axis=0)
    return (
        jnp.asarray(forward, jnp.bfloat16),
        jnp.asarray(backward, jnp.bfloat16),
        jnp.asarray(turn_cos, jnp.float32),
        jnp.asarray(turn_sin, jnp.float32),
    )


def fft_real(xs):
    size = len(xs)
    if size == 1:
        return [(xs[0], None)]
    if size == 2:
        turned = xs[1] * math.cos(math.pi / 4)
        return [(xs[0] + turned, -turned), (xs[0] - turned, turned)]
    even, odd = fft_real(xs[0::2]), fft_real(xs[1::2])
    low, high = [], []
    for k in range(size // 2):
        angle = -2.0 * math.pi * (k + 0.25) / size
        cos, sin = math.cos(angle), math.sin(angle)
        (er, ei), (orr, oi) = even[k], odd[k]
        tr = orr * cos - oi * sin
        ti = orr * sin + oi * cos
        low.append((er + tr, ei + ti))
        high.append((er - tr, ei - ti))
    return low + high


def fft_back(pairs):
    size = len(pairs)
    if size == 2:
        (ar, ai), (br, bi) = pairs
        return [ar + br, ((ar - br) - (ai - bi)) * math.cos(math.pi / 4)]
    half = size // 2
    even, odd = [], []
    for k in range(half):
        angle = 2.0 * math.pi * (k + 0.25) / size
        cos, sin = math.cos(angle), math.sin(angle)
        (ar, ai), (br, bi) = pairs[k], pairs[k + half]
        even.append((ar + br, ai + bi))
        dr, di = ar - br, ai - bi
        odd.append((dr * cos - di * sin, dr * sin + di * cos))
    even, odd = fft_back(even), fft_back(odd)
    return [term for pair in zip(even, odd) for term in pair]


def transforms(devices, group, held, turn_cos, turn_sin):
    cols = held.shape[1]

    def into(spec):
        def step(j, carry):
            xs = [held[pl.ds(n * group + j * 8, 8), :] for n in range(devices)]
            for k, (re, im) in enumerate(fft_real(xs)):
                cos, sin = turn_cos[8 * k : 8 * k + 8, :], turn_sin[8 * k : 8 * k + 8, :]
                at = pl.ds(k * group + j * 8, 8)
                spec[at, :cols] = re * cos - im * sin
                spec[at, cols:] = re * sin + im * cos
            return carry

        lax.fori_loop(0, group // 8, step, 0)

    def outof(spec, scale):
        def step(j, carry):
            pairs = []
            for k in range(devices):
                cos, sin = turn_cos[8 * k : 8 * k + 8, :], turn_sin[8 * k : 8 * k + 8, :]
                at = pl.ds(k * group + j * 8, 8)
                re, im = spec[at, :cols], spec[at, cols:]
                pairs.append((re * cos + im * sin, im * cos - re * sin))
            for n, term in enumerate(fft_back(pairs)):
                held[pl.ds(n * group + j * 8, 8), :] = term * scale
            return carry

        lax.fori_loop(0, group // 8, step, 0)

    return into, outof


def correlate(spec_a, spec_b, spec_c, forward, backward):
    rows, cols = spec_a.shape[0], spec_a.shape[1] // 2
    block = min(rows, 256)

    def step(i, carry):
        at = pl.ds(pl.multiple_of(i * block, block), block)

        def line(spec):
            moved = jnp.dot(spec[at, :].astype(jnp.bfloat16), forward[...], preferred_element_type=jnp.float32)
            return moved[:, :cols], moved[:, cols:]

        ar, ai = line(spec_a)
        for spec in (spec_b, spec_c):
            br, bi = line(spec)
            mixed = jnp.concatenate([ar * br + ai * bi, ai * br - ar * bi], axis=1).astype(jnp.bfloat16)
            spec[at, :] = jnp.dot(mixed, backward[...], preferred_element_type=jnp.float32)
        return carry

    lax.fori_loop(0, rows // block, step, 0)


def fetch(sources, slots, done):
    copies = [pltpu.make_async_copy(source, slot, done.at[i]) for i, (source, slot) in enumerate(zip(sources, slots))]
    for copy in copies:
        copy.start()
    return copies


def begin_kernel(
    square, conv_one, filter_two, filter_one, out_cot, conv_two, block_in, w_out, w_in,
    sent, second_out, late, rows_here, w_out_here, w_in_here, done,
):
    devices, _, group, lanes = sent.shape
    width = out_cot.shape[1]
    copies = fetch(
        [conv_one, filter_two, filter_one, out_cot, w_out, conv_two, block_in] + [w_in.at[:, i * width : (i + 1) * width] for i in (2, 1, 0)],
        [rows_here.at[i] for i in range(4)] + [w_out_here, rows_here.at[4], rows_here.at[5]] + [w_in_here.at[i] for i in (2, 1, 0)],
        done,
    )

    def turned(x):
        parts = [
            lax.dot_general(square[...], x[:, at : at + lanes], LAST, preferred_element_type=jnp.float32)
            for at in range(0, width, lanes)
        ]
        return jnp.concatenate(parts, axis=0).astype(jnp.bfloat16)

    def send(i, x):
        sent[:, i] = turned(x).reshape(devices, group, lanes)

    def project(i):
        return jnp.dot(rows_here[5], w_in_here[i], preferred_element_type=jnp.float32).astype(jnp.bfloat16)

    for i in range(3):
        copies[i].wait()
        send(i, rows_here[i])
    copies[3].wait()
    copies[4].wait()
    grad_second = lax.dot_general(rows_here[3], w_out_here[...], LAST, preferred_element_type=jnp.float32).astype(jnp.bfloat16)
    copies[5].wait()
    grad_gate_two = product(grad_second, rows_here[4])
    late[...] = grad_gate_two
    send(6, grad_gate_two)
    copies[6].wait()
    copies[7].wait()
    gate_two = project(2)
    send(3, product(grad_second, gate_two))
    second_out[...] = turned(product(gate_two, rows_here[4]))
    copies[8].wait()
    send(4, project(1))
    copies[9].wait()
    send(5, project(0))


def middle_kernel(scale, me, here, forward, backward, turn_cos, turn_sin, back, slab, held, spec_a, spec_b, spec_c):
    devices, _, group, cols = here.shape
    rows = devices * group
    into, outof = transforms(devices, group, held, turn_cos, turn_sin)
    flat = lambda i: here[:, i].astype(jnp.float32).reshape(rows, cols)
    blocks = lambda x: x.astype(jnp.bfloat16).reshape(devices, group, cols)

    def lay(kind, x):
        for n in range(devices):
            place = n ^ me[0]
            at = pl.ds(pl.multiple_of(((place & 1) * (devices // 2) + (place >> 1)) * cols, cols), cols)
            slab[kind * group : (kind + 1) * group, at] = x[n * group : (n + 1) * group].astype(slab.dtype)

    held[...] = flat(3)
    into(spec_a)
    held[...] = flat(1)
    into(spec_b)
    held[...] = (flat(4) * flat(0)).astype(jnp.bfloat16).astype(jnp.float32)
    into(spec_c)
    correlate(spec_a, spec_b, spec_c, forward, backward)
    outof(spec_c, scale)
    back[:, 3] = blocks(held[...])
    outof(spec_b, scale)
    grad_first = held[...].astype(jnp.bfloat16).astype(jnp.float32)
    gate_grad = grad_first * flat(0)
    back[:, 1] = blocks(gate_grad)
    lay(1, gate_grad)
    held[...] = (grad_first * flat(4)).astype(jnp.bfloat16).astype(jnp.float32)
    into(spec_a)
    held[...] = flat(2)
    into(spec_b)
    held[...] = flat(5)
    into(spec_c)
    lay(2, flat(6))
    slab[3 * group :, :] = jnp.zeros((cols - 3 * group, devices * cols), slab.dtype)
    correlate(spec_a, spec_b, spec_c, forward, backward)
    outof(spec_c, scale)
    back[:, 2] = blocks(held[...])
    outof(spec_b, scale)
    back[:, 0] = blocks(held[...])
    lay(0, held[...])


def slab_kernel(scale, slab, *refs):
    *pieces, part, slots, done = refs
    count, (depth, steps, width) = len(pieces), slots.shape
    devices, group, cols = part.shape
    copies = [pltpu.make_async_copy(piece, slots.at[i % depth], done.at[i]) for i, piece in enumerate(pieces)]
    for copy in copies[:depth]:
        copy.start()
    total = jnp.zeros((cols, width), jnp.float32)
    for i, copy in enumerate(copies):
        copy.wait()
        total += jnp.dot(slab[:, i * steps : (i + 1) * steps], slots[i % depth], preferred_element_type=jnp.float32)
        if i + depth < count:
            copies[i + depth].start()
    part[...] = (total * scale).T.astype(jnp.bfloat16).reshape(devices, group, cols)


def on_chip(kernel, out_shape, args, scratch=(), far=(), vmem_mib=48):
    vmem = pl.BlockSpec(memory_space=pltpu.VMEM)
    spaces = [pltpu.SMEM if x.dtype == jnp.int32 else pltpu.HBM if i in far else pltpu.VMEM for i, x in enumerate(args)]
    return pl.pallas_call(
        kernel,
        out_shape=out_shape,
        in_specs=[pl.BlockSpec(memory_space=space) for space in spaces],
        out_specs=jax.tree.map(lambda _: vmem, out_shape),
        scratch_shapes=list(scratch),
        compiler_params=pltpu.CompilerParams(vmem_limit_bytes=vmem_mib * 2**20),
    )(*args)


def long_convs(rows, rows_dev):
    spec = pltpu.VMEM((rows, 2 * rows_dev), jnp.float32)
    return [pltpu.VMEM((rows, rows_dev), jnp.float32), spec, spec, spec]


def home_kernel(square, home, part, w_in, in_grad, filter_one_grad, filter_two_grad, home_here, part_here, w_in_here, done):
    devices, _, group, lanes = home.shape
    width = devices * group
    copies = fetch(
        [home, part] + [w_in.at[:, i * width : (i + 1) * width] for i in range(2)],
        [home_here, part_here] + [w_in_here.at[i] for i in range(2)],
        done,
    )

    def whole(i):
        field = home_here[:, i].astype(jnp.float32).reshape(width, lanes).astype(jnp.bfloat16)
        return lax.dot_general(square[...], field, LAST, preferred_element_type=jnp.float32).astype(jnp.bfloat16)

    copies[0].wait()
    filter_one_grad[...] = whole(2)
    filter_two_grad[...] = whole(3)
    copies[1].wait()
    total = part_here[...]
    for i in (0, 1):
        copies[2 + i].wait()
        total += lax.dot_general(whole(i), w_in_here[i], LAST, preferred_element_type=jnp.float32)
    in_grad[...] = total.astype(jnp.bfloat16)


def place_kernel(taken, moves, w_in_grad):
    devices, group, lanes = taken.shape
    per, kinds = moves.shape[0], moves.shape[2] // lanes
    for g in range(devices // per):
        total = jnp.zeros((group, kinds * lanes), jnp.float32)
        for s in range(per):
            total += jnp.dot(taken[g * per + s], moves[s], preferred_element_type=jnp.float32)
        for f in range(kinds):
            at = f * devices * group + g * lanes
            w_in_grad[:, at : at + lanes] = total[:, f * lanes : (f + 1) * lanes]


def moves_of(group, lanes, kinds):
    per = lanes // group
    table = np.zeros((per, lanes, kinds * lanes), np.float32)
    for s in range(per):
        for f in range(kinds):
            for c in range(group):
                table[s, f * group + c, f * lanes + s * group + c] = 1.0
    return jnp.asarray(table, jnp.bfloat16)


def bits_of(count):
    return [1 << i for i in range(count.bit_length() - 1)]


def swap(block, axis, bit):
    return lax.ppermute(block, axis, [(i, i ^ bit) for i in range(lax.axis_size(axis))])


def after(x, *others):
    return lax.optimization_barrier((x, *others))[0]


def chips_of(block):
    blocks = [block] + [None] * (lax.axis_size("minor") // 2 - 1)
    for j in range(len(blocks) - 1, 0, -1):
        if j & (j - 1) == 0:
            blocks[j] = swap(block, "minor", 2 * j)
    return blocks


def far_chips(blocks, later):
    blocks = list(blocks)
    for j in range(1, len(blocks)):
        low = j & -j
        if j != low:
            blocks[j] = swap(after(blocks[j ^ low], later), "minor", 2 * low)
    return blocks


def major_near(blocks):
    half = max(len(blocks) // 2, 1)
    lines = []
    for part in (blocks[:half], blocks[half:]):
        whole = jnp.concatenate(part)
        held = [whole] + [None] * (lax.axis_size("major") - 1)
        for j in range(1, len(held)):
            if j & (j - 1) == 0:
                held[j] = swap(whole, "major", j)
        lines.append(held)
    return lines


def gather_chips(lines, later):
    pieces = []
    for turn, line in enumerate(lines):
        held = [piece if piece is None else after(piece, later) for piece in line]
        for j in range(1, len(held)):
            bit = j & -j if turn else 1 << (j.bit_length() - 1)
            if j != bit:
                held[j] = swap(held[j ^ bit], "major", bit)
        pieces.append(held)
    return [piece for pair in zip(*pieces) for piece in pair]


def out_part(second_out, cots):
    width, rows_dev = second_out.shape
    majors, minors = lax.axis_size("major"), lax.axis_size("minor")
    mine = lax.axis_index("major")
    slabs = second_out.reshape(majors, width // majors, rows_dev)
    slab = [lax.dynamic_index_in_dim(slabs, mine ^ j, 0, keepdims=False) for j in range(majors)]
    slab = jnp.stack([swap(part, "major", j) if j else part for j, part in enumerate(slab)])
    total = jnp.einsum("mct,mtw->cw", slab, jnp.stack(cots), preferred_element_type=jnp.float32)
    total = total.reshape(minors // 2, 2, -1, total.shape[1])
    mine = lax.axis_index("minor") % 2
    part = lambda core: lax.dynamic_index_in_dim(total, core, 1, keepdims=False)
    return part(mine) + swap(part(1 - mine), "minor", 1)


def out_parts(total):
    mine = lax.axis_index("minor") // 2
    part = lambda chip: lax.dynamic_index_in_dim(total, chip, 0, keepdims=False)
    return [part(mine)] + [swap(part(mine ^ j).astype(jnp.bfloat16), "minor", 2 * j) for j in range(1, total.shape[0])]


def regroup(x):
    return lax.all_to_all(x, AXES, split_axis=0, concat_axis=0, tiled=True)


def shards(block_in, out_cot, w_in, w_out, conv_one, conv_two, filter_one, filter_two):
    rows_dev, width = block_in.shape
    devices, majors = lax.axis_size(AXES), lax.axis_size("major")
    group = width // devices
    scale = (rows_dev * devices) ** (-0.5)
    fft_scale = scale / (rows_dev * devices)
    field = lambda *dims: jax.ShapeDtypeStruct((devices, *dims, group, rows_dev), jnp.bfloat16)
    array = lambda *dims: jax.ShapeDtypeStruct(dims, jnp.bfloat16)

    near_in = chips_of(block_in)
    square = jnp.eye(rows_dev, dtype=jnp.bfloat16)
    sent, second_out, late = on_chip(
        begin_kernel,
        [field(7), array(width, rows_dev), array(rows_dev, width)],
        (square, conv_one, filter_two, filter_one, out_cot, conv_two, block_in, w_out, w_in),
        [
            pltpu.VMEM((6, rows_dev, width), jnp.bfloat16),
            pltpu.VMEM((width, width), jnp.bfloat16),
            pltpu.VMEM((3, width, width), jnp.bfloat16),
            pltpu.SemaphoreType.DMA((10,)),
        ],
        range(1, 9),
        60,
    )
    cots = [swap(out_cot, "major", j) if j else out_cot for j in range(majors)]
    near_in = far_chips(near_in, late)
    sent = after(sent, *cots, *near_in)
    here = regroup(sent)
    total = out_part(after(second_out, sent), cots)
    late = lax.dot_general(late, w_in[:, 2 * width :], LAST, preferred_element_type=jnp.float32)
    lines = major_near([after(block, sent) for block in near_in])
    here = after(here, late, total, *[piece for line in lines for piece in line if piece is not None])

    spec = pltpu.VMEM((devices * group, 2 * rows_dev), jnp.float32)
    back, slab = on_chip(
        functools.partial(middle_kernel, fft_scale),
        [field(4), array(rows_dev, devices * rows_dev)],
        (lax.axis_index(AXES).astype(jnp.int32)[None], here, *tables(devices, rows_dev)),
        [pltpu.VMEM((devices * group, rows_dev), jnp.float32), spec, spec, spec],
    )
    all_in = gather_chips(lines, here)
    parts = out_parts(after(total, *[piece for piece in lines[0] if piece is not None]))
    back, *parts = lax.optimization_barrier((back, *parts, *all_in))[: 1 + len(parts)]
    w_out_grad = sum(part.astype(jnp.float32) for part in parts) * scale
    home = regroup(back)
    all_in += [swap(after(piece, back), "minor", 1) for piece in all_in]

    rows = all_in[0].shape[0]
    slots = min(len(all_in), 16 * 2**20 // (2 * rows * width))
    part = on_chip(
        functools.partial(slab_kernel, scale),
        field(),
        (slab, *all_in),
        [pltpu.VMEM((slots, rows, width), jnp.bfloat16), pltpu.SemaphoreType.DMA((len(all_in),))],
        range(1, 1 + len(all_in)),
        60,
    )
    taken = regroup(after(part, home))
    in_grad, filter_one_grad, filter_two_grad = on_chip(
        home_kernel,
        [array(rows_dev, width)] * 3,
        (square, home, late, w_in),
        [
            pltpu.VMEM(home.shape, jnp.bfloat16),
            pltpu.VMEM((rows_dev, width), jnp.float32),
            pltpu.VMEM((2, width, width), jnp.bfloat16),
            pltpu.SemaphoreType.DMA((4,)),
        ],
        range(1, 4),
        60,
    )
    w_in_grad = on_chip(
        place_kernel, jax.ShapeDtypeStruct((group, 3 * width), jnp.float32), (taken, moves_of(group, rows_dev, 3))
    )
    return in_grad, w_in_grad, w_out_grad, filter_one_grad, filter_two_grad


def solution(mesh):
    tokens = P(AXES, None)
    return jax.shard_map(
        shards,
        mesh=mesh,
        in_specs=(tokens, tokens, P(), P(), tokens, tokens, tokens, tokens),
        out_specs=(tokens,) * 5,
        check_vma=False,
    )
```

```python
import functools
import math

import jax
import jax.numpy as jnp
import numpy as np
from jax import lax
from jax.experimental import pallas as pl
from jax.experimental.pallas import tpu as pltpu
from jax.sharding import PartitionSpec as P

AXES = ("major", "minor")
LAST = (((1,), (1,)), ((), ()))


def product(left, right):
    return (left.astype(jnp.float32) * right.astype(jnp.float32)).astype(jnp.bfloat16)


def tables(devices, rows_dev):
    seq_len = devices * rows_dev
    line = np.arange(rows_dev)
    angle = -2.0 * math.pi * (line[:, None] * line[None, :] % rows_dev) / rows_dev
    cos, sin = np.cos(angle), np.sin(angle)
    forward = np.block([[cos, sin], [-sin, cos]])
    backward = np.block([[cos, -sin], [sin, cos]])
    turn = -2.0 * math.pi * (np.arange(devices)[:, None] + 0.25) * line[None, :] / seq_len
    turn_cos = np.repeat(np.cos(turn), 8, axis=0)
    turn_sin = np.repeat(np.sin(turn), 8, axis=0)
    return (
        jnp.asarray(forward, jnp.bfloat16),
        jnp.asarray(backward, jnp.bfloat16),
        jnp.asarray(turn_cos, jnp.float32),
        jnp.asarray(turn_sin, jnp.float32),
    )


def turned_by(pair, step, size):
    re, im = pair
    step %= size
    if step == 0:
        return pair
    if 4 * step == size:
        return im, -re
    if 2 * step == size:
        return -re, -im
    if 4 * step == 3 * size:
        return -im, re
    cos, sin = math.cos(2.0 * math.pi * step / size), math.sin(2.0 * math.pi * step / size)
    if 8 * step == size:
        return (re + im) * cos, (im - re) * cos
    if 8 * step == 3 * size:
        return (im - re) * sin, -(re + im) * sin
    if 8 * step == 5 * size:
        return (re + im) * cos, (im - re) * cos
    if 8 * step == 7 * size:
        return (re - im) * cos, (im + re) * cos
    return re * cos + im * sin, im * cos - re * sin


def fft(pairs):
    size = len(pairs)
    if size == 1:
        return pairs
    even, odd = fft(pairs[0::2]), fft(pairs[1::2])
    low, high = [], []
    for k in range(size // 2):
        (er, ei), (tr, ti) = even[k], turned_by(odd[k], k, size)
        low.append((er + tr, ei + ti))
        high.append((er - tr, ei - ti))
    return low + high


def fft_real(xs):
    angles = [2.0 * math.pi * n / (4 * len(xs)) for n in range(len(xs))]
    return fft([(x * math.cos(angle), x * -math.sin(angle)) for x, angle in zip(xs, angles)])


def fft_back(pairs):
    def sums(pairs):
        size = len(pairs)
        if size == 1:
            return pairs
        half = size // 2
        even, odd = [], []
        for k in range(half):
            (ar, ai), (br, bi) = pairs[k], pairs[k + half]
            even.append((ar + br, ai + bi))
            odd.append(turned_by((ar - br, ai - bi), -k, size))
        return [term for pair in zip(sums(even), sums(odd)) for term in pair]

    angles = [2.0 * math.pi * n / (4 * len(pairs)) for n in range(len(pairs))]
    return [re * math.cos(angle) - im * math.sin(angle) for (re, im), angle in zip(sums(pairs), angles)]


def transforms(devices, group, held, turn_cos, turn_sin):
    cols = held.shape[1]

    def into(spec):
        def step(j, carry):
            xs = [held[pl.ds(n * group + j * 8, 8), :] for n in range(devices)]
            for k, (re, im) in enumerate(fft_real(xs)):
                cos, sin = turn_cos[8 * k : 8 * k + 8, :], turn_sin[8 * k : 8 * k + 8, :]
                at = pl.ds(k * group + j * 8, 8)
                spec[at, :cols] = re * cos - im * sin
                spec[at, cols:] = re * sin + im * cos
            return carry

        lax.fori_loop(0, group // 8, step, 0)

    def outof(spec, scale):
        def step(j, carry):
            pairs = []
            for k in range(devices):
                cos, sin = turn_cos[8 * k : 8 * k + 8, :], turn_sin[8 * k : 8 * k + 8, :]
                at = pl.ds(k * group + j * 8, 8)
                re, im = spec[at, :cols], spec[at, cols:]
                pairs.append((re * cos + im * sin, im * cos - re * sin))
            for n, term in enumerate(fft_back(pairs)):
                held[pl.ds(n * group + j * 8, 8), :] = term * scale
            return carry

        lax.fori_loop(0, group // 8, step, 0)

    return into, outof


def correlate(spec_a, spec_b, spec_c, forward, backward):
    rows, cols = spec_a.shape[0], spec_a.shape[1] // 2
    block = min(rows, 256)

    def step(i, carry):
        at = pl.ds(pl.multiple_of(i * block, block), block)

        def line(spec):
            moved = jnp.dot(spec[at, :].astype(jnp.bfloat16), forward[...], preferred_element_type=jnp.float32)
            return moved[:, :cols], moved[:, cols:]

        ar, ai = line(spec_a)
        for spec in (spec_b, spec_c):
            br, bi = line(spec)
            mixed = jnp.concatenate([ar * br + ai * bi, ai * br - ar * bi], axis=1).astype(jnp.bfloat16)
            spec[at, :] = jnp.dot(mixed, backward[...], preferred_element_type=jnp.float32)
        return carry

    lax.fori_loop(0, rows // block, step, 0)


def fetch(sources, slots, done):
    copies = [pltpu.make_async_copy(source, slot, done.at[i]) for i, (source, slot) in enumerate(zip(sources, slots))]
    for copy in copies:
        copy.start()
    return copies


def begin_kernel(
    square, conv_one, filter_two, filter_one, out_cot, conv_two, block_in, w_out, w_in,
    sent, second_out, late, rows_here, w_out_here, w_in_here, done,
):
    devices, _, group, lanes = sent.shape
    width = out_cot.shape[1]
    copies = fetch(
        [conv_one, filter_two, filter_one, out_cot, w_out, conv_two, block_in] + [w_in.at[:, i * width : (i + 1) * width] for i in (2, 1, 0)],
        [rows_here.at[i] for i in range(4)] + [w_out_here, rows_here.at[4], rows_here.at[5]] + [w_in_here.at[i] for i in (2, 1, 0)],
        done,
    )

    def turned(x):
        parts = [
            lax.dot_general(square[...], x[:, at : at + lanes], LAST, preferred_element_type=jnp.float32)
            for at in range(0, width, lanes)
        ]
        return jnp.concatenate(parts, axis=0).astype(jnp.bfloat16)

    def send(i, x):
        sent[:, i] = turned(x).reshape(devices, group, lanes)

    def project(i):
        return jnp.dot(rows_here[5], w_in_here[i], preferred_element_type=jnp.float32).astype(jnp.bfloat16)

    for i in range(3):
        copies[i].wait()
        send(i, rows_here[i])
    copies[3].wait()
    copies[4].wait()
    grad_second = lax.dot_general(rows_here[3], w_out_here[...], LAST, preferred_element_type=jnp.float32).astype(jnp.bfloat16)
    copies[5].wait()
    grad_gate_two = product(grad_second, rows_here[4])
    late[...] = grad_gate_two
    send(6, grad_gate_two)
    copies[6].wait()
    copies[7].wait()
    gate_two = project(2)
    send(3, product(grad_second, gate_two))
    second_out[...] = turned(product(gate_two, rows_here[4]))
    copies[8].wait()
    send(4, project(1))
    copies[9].wait()
    send(5, project(0))


def middle_kernel(scale, me, here, forward, backward, turn_cos, turn_sin, back_far, slab, held, spec_a, spec_b, spec_c, back, done):
    devices, _, group, cols = here.shape
    rows = devices * group
    copies = [pltpu.make_async_copy(back.at[:, i], back_far.at[:, i], done.at[i]) for i in range(4)]
    into, outof = transforms(devices, group, held, turn_cos, turn_sin)
    flat = lambda i: here[:, i].astype(jnp.float32).reshape(rows, cols)
    blocks = lambda x: x.astype(jnp.bfloat16).reshape(devices, group, cols)

    def lay(kind, x):
        for n in range(devices):
            place = n ^ me[0]
            at = pl.ds(pl.multiple_of(((place & 1) * (devices // 2) + (place >> 1)) * cols, cols), cols)
            slab[kind * group : (kind + 1) * group, at] = x[n * group : (n + 1) * group].astype(slab.dtype)

    held[...] = flat(3)
    into(spec_a)
    held[...] = flat(1)
    into(spec_b)
    held[...] = (flat(4) * flat(0)).astype(jnp.bfloat16).astype(jnp.float32)
    into(spec_c)
    correlate(spec_a, spec_b, spec_c, forward, backward)
    outof(spec_c, scale)
    back[:, 3] = blocks(held[...])
    copies[3].start()
    outof(spec_b, scale)
    grad_first = held[...].astype(jnp.bfloat16).astype(jnp.float32)
    gate_grad = grad_first * flat(0)
    back[:, 1] = blocks(gate_grad)
    copies[1].start()
    lay(1, gate_grad)
    held[...] = (grad_first * flat(4)).astype(jnp.bfloat16).astype(jnp.float32)
    into(spec_a)
    held[...] = flat(2)
    into(spec_b)
    held[...] = flat(5)
    into(spec_c)
    lay(2, flat(6))
    slab[3 * group :, :] = jnp.zeros((cols - 3 * group, devices * cols), slab.dtype)
    correlate(spec_a, spec_b, spec_c, forward, backward)
    outof(spec_c, scale)
    back[:, 2] = blocks(held[...])
    copies[2].start()
    outof(spec_b, scale)
    back[:, 0] = blocks(held[...])
    copies[0].start()
    lay(0, held[...])
    for copy in copies:
        copy.wait()


def slab_kernel(scale, slab, *refs):
    *pieces, part, slots, done = refs
    count, (depth, steps, width) = len(pieces), slots.shape
    devices, group, cols = part.shape
    copies = [pltpu.make_async_copy(piece, slots.at[i % depth], done.at[i]) for i, piece in enumerate(pieces)]
    for copy in copies[:depth]:
        copy.start()
    total = jnp.zeros((cols, width), jnp.float32)
    for i, copy in enumerate(copies):
        copy.wait()
        total += jnp.dot(slab[:, i * steps : (i + 1) * steps], slots[i % depth], preferred_element_type=jnp.float32)
        if i + depth < count:
            copies[i + depth].start()
    part[...] = (total * scale).T.astype(jnp.bfloat16).reshape(devices, group, cols)


def on_chip(kernel, out_shape, args, scratch=(), far=(), vmem_mib=48, far_out=()):
    alone = not isinstance(out_shape, list)
    out_shape = [out_shape] if alone else out_shape
    spaces = [pltpu.SMEM if x.dtype == jnp.int32 else pltpu.HBM if i in far else pltpu.VMEM for i, x in enumerate(args)]
    outs = pl.pallas_call(
        kernel,
        out_shape=out_shape,
        in_specs=[pl.BlockSpec(memory_space=space) for space in spaces],
        out_specs=[pl.BlockSpec(memory_space=pltpu.HBM if i in far_out else pltpu.VMEM) for i in range(len(out_shape))],
        scratch_shapes=list(scratch),
        compiler_params=pltpu.CompilerParams(vmem_limit_bytes=vmem_mib * 2**20),
    )(*args)
    return outs[0] if alone else outs


def long_convs(rows, rows_dev):
    spec = pltpu.VMEM((rows, 2 * rows_dev), jnp.float32)
    return [pltpu.VMEM((rows, rows_dev), jnp.float32), spec, spec, spec]


def home_kernel(square, home, part, w_in, in_grad, filter_one_grad, filter_two_grad, home_here, part_here, w_in_here, done):
    devices, _, group, lanes = home.shape
    width = devices * group
    copies = fetch(
        [home, part] + [w_in.at[:, i * width : (i + 1) * width] for i in range(2)],
        [home_here, part_here] + [w_in_here.at[i] for i in range(2)],
        done,
    )

    def whole(i):
        field = home_here[:, i].astype(jnp.float32).reshape(width, lanes).astype(jnp.bfloat16)
        return lax.dot_general(square[...], field, LAST, preferred_element_type=jnp.float32).astype(jnp.bfloat16)

    copies[0].wait()
    filter_one_grad[...] = whole(2)
    filter_two_grad[...] = whole(3)
    copies[1].wait()
    total = part_here[...]
    for i in (0, 1):
        copies[2 + i].wait()
        total += lax.dot_general(whole(i), w_in_here[i], LAST, preferred_element_type=jnp.float32)
    in_grad[...] = total.astype(jnp.bfloat16)


def place_kernel(taken, moves, w_in_grad):
    devices, group, lanes = taken.shape
    per, kinds = moves.shape[0], moves.shape[2] // lanes
    for g in range(devices // per):
        total = jnp.zeros((group, kinds * lanes), jnp.float32)
        for s in range(per):
            total += jnp.dot(taken[g * per + s], moves[s], preferred_element_type=jnp.float32)
        for f in range(kinds):
            at = f * devices * group + g * lanes
            w_in_grad[:, at : at + lanes] = total[:, f * lanes : (f + 1) * lanes]


def moves_of(group, lanes, kinds):
    per = lanes // group
    table = np.zeros((per, lanes, kinds * lanes), np.float32)
    for s in range(per):
        for f in range(kinds):
            for c in range(group):
                table[s, f * group + c, f * lanes + s * group + c] = 1.0
    return jnp.asarray(table, jnp.bfloat16)


def bits_of(count):
    return [1 << i for i in range(count.bit_length() - 1)]


def swap(block, axis, bit):
    return lax.ppermute(block, axis, [(i, i ^ bit) for i in range(lax.axis_size(axis))])


def after(x, *others):
    return lax.optimization_barrier((x, *others))[0]


def chips_of(block):
    blocks = [block] + [None] * (lax.axis_size("minor") // 2 - 1)
    for j in range(len(blocks) - 1, 0, -1):
        if j & (j - 1) == 0:
            blocks[j] = swap(block, "minor", 2 * j)
    return blocks


def far_chips(blocks, later):
    blocks, first = list(blocks), []
    for j in range(1, len(blocks)):
        low = j & -j
        if j != low:
            block = after(blocks[j ^ low], later)
            first.append(swap(block[:16], "minor", 2 * low))
            blocks[j] = jnp.concatenate([first[-1], swap(block[16:], "minor", 2 * low)])
    return blocks, first


def major_near(blocks):
    half = max(len(blocks) // 2, 1)
    lines = []
    for part in (blocks[:half], blocks[half:]):
        whole = jnp.concatenate(part)
        held = [whole] + [None] * (lax.axis_size("major") - 1)
        for j in range(1, len(held)):
            if j & (j - 1) == 0:
                held[j] = swap(whole, "major", j)
        lines.append(held)
    return lines


def gather_chips(lines, later):
    pieces = []
    for turn, line in enumerate(lines):
        held = [piece if piece is None else after(piece, later) for piece in line]
        for j in range(1, len(held)):
            bit = j & -j if turn else 1 << (j.bit_length() - 1)
            if j != bit:
                held[j] = swap(held[j ^ bit], "major", bit)
        pieces.append(held)
    return [piece for pair in zip(*pieces) for piece in pair]


def out_part(second_out, cots):
    width, rows_dev = second_out.shape
    majors, minors = lax.axis_size("major"), lax.axis_size("minor")
    mine = lax.axis_index("major")
    slabs = second_out.reshape(majors, width // majors, rows_dev)
    slab = [lax.dynamic_index_in_dim(slabs, mine ^ j, 0, keepdims=False) for j in range(majors)]
    slab = jnp.stack([swap(part, "major", j) if j else part for j, part in enumerate(slab)])
    total = jnp.einsum("mct,mtw->cw", slab, jnp.stack(cots), preferred_element_type=jnp.float32)
    total = total.reshape(minors // 2, 2, -1, total.shape[1])
    mine = lax.axis_index("minor") % 2
    part = lambda core: lax.dynamic_index_in_dim(total, core, 1, keepdims=False)
    return part(mine) + swap(part(1 - mine), "minor", 1)


def out_parts(total):
    mine = lax.axis_index("minor") // 2
    part = lambda chip: lax.dynamic_index_in_dim(total, chip, 0, keepdims=False)
    return [part(mine)] + [swap(part(mine ^ j).astype(jnp.bfloat16), "minor", 2 * j) for j in range(1, total.shape[0])]


def regroup(x):
    return lax.all_to_all(x, AXES, split_axis=0, concat_axis=0, tiled=True)


def shards(block_in, out_cot, w_in, w_out, conv_one, conv_two, filter_one, filter_two):
    rows_dev, width = block_in.shape
    devices, majors = lax.axis_size(AXES), lax.axis_size("major")
    group = width // devices
    scale = (rows_dev * devices) ** (-0.5)
    fft_scale = scale / (rows_dev * devices)
    field = lambda *dims: jax.ShapeDtypeStruct((devices, *dims, group, rows_dev), jnp.bfloat16)
    array = lambda *dims: jax.ShapeDtypeStruct(dims, jnp.bfloat16)

    near_in = chips_of(block_in)
    square = jnp.eye(rows_dev, dtype=jnp.bfloat16)
    sent, second_out, late = on_chip(
        begin_kernel,
        [field(7), array(width, rows_dev), array(rows_dev, width)],
        (square, conv_one, filter_two, filter_one, out_cot, conv_two, block_in, w_out, w_in),
        [
            pltpu.VMEM((6, rows_dev, width), jnp.bfloat16),
            pltpu.VMEM((width, width), jnp.bfloat16),
            pltpu.VMEM((3, width, width), jnp.bfloat16),
            pltpu.SemaphoreType.DMA((10,)),
        ],
        range(1, 9),
        60,
    )
    cots = [swap(out_cot, "major", j) if j else out_cot for j in range(majors)]
    sent = after(sent, *cots, *[block for block in near_in if block is not None])
    near_in, first = far_chips(near_in, late)
    sent = after(sent, *first)
    here = regroup(sent)
    total = out_part(after(second_out, sent), cots)
    late = lax.dot_general(late, w_in[:, 2 * width :], LAST, preferred_element_type=jnp.float32)
    lines = major_near([after(block, sent) for block in near_in])
    here = after(here, late, total, *[piece for line in lines for piece in line if piece is not None])

    spec = pltpu.VMEM((devices * group, 2 * rows_dev), jnp.float32)
    back, slab = on_chip(
        functools.partial(middle_kernel, fft_scale),
        [field(4), array(rows_dev, devices * rows_dev)],
        (lax.axis_index(AXES).astype(jnp.int32)[None], here, *tables(devices, rows_dev)),
        [
            pltpu.VMEM((devices * group, rows_dev), jnp.float32),
            spec,
            spec,
            spec,
            pltpu.VMEM((devices, 4, group, rows_dev), jnp.bfloat16),
            pltpu.SemaphoreType.DMA((4,)),
        ],
        far_out=(0,),
    )
    all_in = gather_chips(lines, here)
    parts = out_parts(after(total, *[piece for piece in lines[0] if piece is not None]))
    back, *parts = lax.optimization_barrier((back, *parts, *all_in))[: 1 + len(parts)]
    w_out_grad = sum(part.astype(jnp.float32) for part in parts) * scale
    home = regroup(back)
    all_in += [swap(after(piece, back), "minor", 1) for piece in all_in]

    rows = all_in[0].shape[0]
    slots = min(len(all_in), 16 * 2**20 // (2 * rows * width))
    part = on_chip(
        functools.partial(slab_kernel, scale),
        field(),
        (slab, *all_in),
        [pltpu.VMEM((slots, rows, width), jnp.bfloat16), pltpu.SemaphoreType.DMA((len(all_in),))],
        range(1, 1 + len(all_in)),
        60,
    )
    taken = regroup(after(part, home))
    in_grad, filter_one_grad, filter_two_grad = on_chip(
        home_kernel,
        [array(rows_dev, width)] * 3,
        (square, home, late, w_in),
        [
            pltpu.VMEM(home.shape, jnp.bfloat16),
            pltpu.VMEM((rows_dev, width), jnp.float32),
            pltpu.VMEM((2, width, width), jnp.bfloat16),
            pltpu.SemaphoreType.DMA((4,)),
        ],
        range(1, 4),
        60,
    )
    w_in_grad = on_chip(
        place_kernel, jax.ShapeDtypeStruct((group, 3 * width), jnp.float32), (taken, moves_of(group, rows_dev, 3))
    )
    return in_grad, w_in_grad, w_out_grad, filter_one_grad, filter_two_grad


def solution(mesh):
    tokens = P(AXES, None)
    return jax.shard_map(
        shards,
        mesh=mesh,
        in_specs=(tokens, tokens, P(), P(), tokens, tokens, tokens, tokens),
        out_specs=(tokens,) * 5,
        check_vma=False,
    )
```

```python
import functools
import math

import jax
import jax.numpy as jnp
import numpy as np
from jax import lax
from jax.experimental import pallas as pl
from jax.experimental.pallas import tpu as pltpu
from jax.sharding import PartitionSpec as P

AXES = ("major", "minor")
LAST = (((1,), (1,)), ((), ()))


def product(left, right):
    return (left.astype(jnp.float32) * right.astype(jnp.float32)).astype(jnp.bfloat16)


def tables(devices, rows_dev):
    seq_len = devices * rows_dev
    line = np.arange(rows_dev)
    angle = -2.0 * math.pi * (line[:, None] * line[None, :] % rows_dev) / rows_dev
    cos, sin = np.cos(angle), np.sin(angle)
    forward = np.block([[cos, sin], [-sin, cos]])
    backward = np.block([[cos, -sin], [sin, cos]])
    turn = -2.0 * math.pi * (np.arange(devices)[:, None] + 0.25) * line[None, :] / seq_len
    turn_cos = np.repeat(np.cos(turn), 8, axis=0)
    turn_sin = np.repeat(np.sin(turn), 8, axis=0)
    return (
        jnp.asarray(forward, jnp.bfloat16),
        jnp.asarray(backward, jnp.bfloat16),
        jnp.asarray(turn_cos, jnp.float32),
        jnp.asarray(turn_sin, jnp.float32),
    )


def turned_by(pair, step, size):
    re, im = pair
    step %= size
    if step == 0:
        return pair
    if 4 * step == size:
        return im, -re
    if 2 * step == size:
        return -re, -im
    if 4 * step == 3 * size:
        return -im, re
    cos, sin = math.cos(2.0 * math.pi * step / size), math.sin(2.0 * math.pi * step / size)
    if 8 * step == size:
        return (re + im) * cos, (im - re) * cos
    if 8 * step == 3 * size:
        return (im - re) * sin, -(re + im) * sin
    if 8 * step == 5 * size:
        return (re + im) * cos, (im - re) * cos
    if 8 * step == 7 * size:
        return (re - im) * cos, (im + re) * cos
    return re * cos + im * sin, im * cos - re * sin


def fft(pairs):
    size = len(pairs)
    if size == 1:
        return pairs
    even, odd = fft(pairs[0::2]), fft(pairs[1::2])
    low, high = [], []
    for k in range(size // 2):
        (er, ei), (tr, ti) = even[k], turned_by(odd[k], k, size)
        low.append((er + tr, ei + ti))
        high.append((er - tr, ei - ti))
    return low + high


def fft_real(xs):
    angles = [2.0 * math.pi * n / (4 * len(xs)) for n in range(len(xs))]
    return fft([(x * math.cos(angle), x * -math.sin(angle)) for x, angle in zip(xs, angles)])


def fft_back(pairs):
    def sums(pairs):
        size = len(pairs)
        if size == 1:
            return pairs
        half = size // 2
        even, odd = [], []
        for k in range(half):
            (ar, ai), (br, bi) = pairs[k], pairs[k + half]
            even.append((ar + br, ai + bi))
            odd.append(turned_by((ar - br, ai - bi), -k, size))
        return [term for pair in zip(sums(even), sums(odd)) for term in pair]

    angles = [2.0 * math.pi * n / (4 * len(pairs)) for n in range(len(pairs))]
    return [re * math.cos(angle) - im * math.sin(angle) for (re, im), angle in zip(sums(pairs), angles)]


def transforms(devices, group, held, turn_cos, turn_sin):
    cols = held.shape[1]

    def into(spec):
        def step(j, carry):
            xs = [held[pl.ds(n * group + j * 8, 8), :] for n in range(devices)]
            for k, (re, im) in enumerate(fft_real(xs)):
                cos, sin = turn_cos[8 * k : 8 * k + 8, :], turn_sin[8 * k : 8 * k + 8, :]
                at = pl.ds(k * group + j * 8, 8)
                spec[at, :cols] = re * cos - im * sin
                spec[at, cols:] = re * sin + im * cos
            return carry

        lax.fori_loop(0, group // 8, step, 0)

    def outof(spec, scale):
        def step(j, carry):
            pairs = []
            for k in range(devices):
                cos, sin = turn_cos[8 * k : 8 * k + 8, :], turn_sin[8 * k : 8 * k + 8, :]
                at = pl.ds(k * group + j * 8, 8)
                re, im = spec[at, :cols], spec[at, cols:]
                pairs.append((re * cos + im * sin, im * cos - re * sin))
            for n, term in enumerate(fft_back(pairs)):
                held[pl.ds(n * group + j * 8, 8), :] = term * scale
            return carry

        lax.fori_loop(0, group // 8, step, 0)

    return into, outof


def correlate(spec_a, spec_b, spec_c, forward, backward):
    rows, cols = spec_a.shape[0], spec_a.shape[1] // 2
    block = min(rows, 512)

    def step(i, carry):
        at = pl.ds(pl.multiple_of(i * block, block), block)

        def line(spec):
            moved = jnp.dot(spec[at, :].astype(jnp.bfloat16), forward[...], preferred_element_type=jnp.float32)
            return moved[:, :cols], moved[:, cols:]

        ar, ai = line(spec_a)
        for spec in (spec_b, spec_c):
            br, bi = line(spec)
            mixed = jnp.concatenate([ar * br + ai * bi, ai * br - ar * bi], axis=1).astype(jnp.bfloat16)
            spec[at, :] = jnp.dot(mixed, backward[...], preferred_element_type=jnp.float32)
        return carry

    lax.fori_loop(0, rows // block, step, 0, unroll=True)


def fetch(sources, slots, done):
    copies = [pltpu.make_async_copy(source, slot, done.at[i]) for i, (source, slot) in enumerate(zip(sources, slots))]
    for copy in copies:
        copy.start()
    return copies


def begin_kernel(
    square, conv_one, filter_two, filter_one, out_cot, conv_two, block_in, w_out, w_in,
    sent, second_out, late, rows_here, w_out_here, w_in_here, done,
):
    devices, _, group, lanes = sent.shape
    width = out_cot.shape[1]
    copies = fetch(
        [conv_one, filter_two, filter_one, out_cot, w_out, conv_two, block_in] + [w_in.at[:, i * width : (i + 1) * width] for i in (2, 1, 0)],
        [rows_here.at[i] for i in range(4)] + [w_out_here, rows_here.at[4], rows_here.at[5]] + [w_in_here.at[i] for i in (2, 1, 0)],
        done,
    )

    def turned(x):
        parts = [
            lax.dot_general(square[...], x[:, at : at + lanes], LAST, preferred_element_type=jnp.float32)
            for at in range(0, width, lanes)
        ]
        return jnp.concatenate(parts, axis=0).astype(jnp.bfloat16)

    def send(i, x):
        sent[:, i] = turned(x).reshape(devices, group, lanes)

    def project(i):
        return jnp.dot(rows_here[5], w_in_here[i], preferred_element_type=jnp.float32).astype(jnp.bfloat16)

    for i in range(3):
        copies[i].wait()
        send(i, rows_here[i])
    copies[3].wait()
    copies[4].wait()
    grad_second = lax.dot_general(rows_here[3], w_out_here[...], LAST, preferred_element_type=jnp.float32).astype(jnp.bfloat16)
    copies[5].wait()
    grad_gate_two = product(grad_second, rows_here[4])
    late[...] = grad_gate_two
    send(6, grad_gate_two)
    copies[6].wait()
    copies[7].wait()
    gate_two = project(2)
    send(3, product(grad_second, gate_two))
    second_out[...] = turned(product(gate_two, rows_here[4]))
    copies[8].wait()
    send(4, project(1))
    copies[9].wait()
    send(5, project(0))


def middle_kernel(scale, me, here, forward, backward, turn_cos, turn_sin, back_far, slab, held, spec_a, spec_b, spec_c, back, done):
    devices, _, group, cols = here.shape
    rows = devices * group
    copies = [pltpu.make_async_copy(back.at[:, i], back_far.at[:, i], done.at[i]) for i in range(4)]
    into, outof = transforms(devices, group, held, turn_cos, turn_sin)
    flat = lambda i: here[:, i].astype(jnp.float32).reshape(rows, cols)
    blocks = lambda x: x.astype(jnp.bfloat16).reshape(devices, group, cols)

    def lay(kind, x):
        for n in range(devices):
            place = n ^ me[0]
            at = pl.ds(pl.multiple_of(((place & 1) * (devices // 2) + (place >> 1)) * cols, cols), cols)
            slab[kind * group : (kind + 1) * group, at] = x[n * group : (n + 1) * group].astype(slab.dtype)

    held[...] = flat(3)
    into(spec_a)
    held[...] = flat(1)
    into(spec_b)
    held[...] = (flat(4) * flat(0)).astype(jnp.bfloat16).astype(jnp.float32)
    into(spec_c)
    correlate(spec_a, spec_b, spec_c, forward, backward)
    outof(spec_c, scale)
    back[:, 3] = blocks(held[...])
    copies[3].start()
    outof(spec_b, scale)
    grad_first = held[...].astype(jnp.bfloat16).astype(jnp.float32)
    gate_grad = grad_first * flat(0)
    back[:, 1] = blocks(gate_grad)
    copies[1].start()
    lay(1, gate_grad)
    held[...] = (grad_first * flat(4)).astype(jnp.bfloat16).astype(jnp.float32)
    into(spec_a)
    held[...] = flat(2)
    into(spec_b)
    held[...] = flat(5)
    into(spec_c)
    lay(2, flat(6))
    slab[3 * group :, :] = jnp.zeros((cols - 3 * group, devices * cols), slab.dtype)
    correlate(spec_a, spec_b, spec_c, forward, backward)
    outof(spec_c, scale)
    back[:, 2] = blocks(held[...])
    copies[2].start()
    outof(spec_b, scale)
    back[:, 0] = blocks(held[...])
    copies[0].start()
    lay(0, held[...])
    for copy in copies:
        copy.wait()


def slab_kernel(scale, slab, *refs):
    *pieces, part, slots, done = refs
    count, (depth, steps, width) = len(pieces), slots.shape
    devices, group, cols = part.shape
    copies = [pltpu.make_async_copy(piece, slots.at[i % depth], done.at[i]) for i, piece in enumerate(pieces)]
    for copy in copies[:depth]:
        copy.start()
    total = jnp.zeros((cols, width), jnp.float32)
    for i, copy in enumerate(copies):
        copy.wait()
        total += jnp.dot(slab[:, i * steps : (i + 1) * steps], slots[i % depth], preferred_element_type=jnp.float32)
        if i + depth < count:
            copies[i + depth].start()
    part[...] = (total * scale).T.astype(jnp.bfloat16).reshape(devices, group, cols)


def on_chip(kernel, out_shape, args, scratch=(), far=(), vmem_mib=48, far_out=()):
    alone = not isinstance(out_shape, list)
    out_shape = [out_shape] if alone else out_shape
    spaces = [pltpu.SMEM if x.dtype == jnp.int32 else pltpu.HBM if i in far else pltpu.VMEM for i, x in enumerate(args)]
    outs = pl.pallas_call(
        kernel,
        out_shape=out_shape,
        in_specs=[pl.BlockSpec(memory_space=space) for space in spaces],
        out_specs=[pl.BlockSpec(memory_space=pltpu.HBM if i in far_out else pltpu.VMEM) for i in range(len(out_shape))],
        scratch_shapes=list(scratch),
        compiler_params=pltpu.CompilerParams(vmem_limit_bytes=vmem_mib * 2**20),
    )(*args)
    return outs[0] if alone else outs


def long_convs(rows, rows_dev):
    spec = pltpu.VMEM((rows, 2 * rows_dev), jnp.float32)
    return [pltpu.VMEM((rows, rows_dev), jnp.float32), spec, spec, spec]


def home_kernel(square, home, part, w_in, in_grad, filter_one_grad, filter_two_grad, home_here, part_here, w_in_here, done):
    devices, _, group, lanes = home.shape
    width = devices * group
    copies = fetch(
        [home, part] + [w_in.at[:, i * width : (i + 1) * width] for i in range(2)],
        [home_here, part_here] + [w_in_here.at[i] for i in range(2)],
        done,
    )

    def whole(i):
        field = home_here[:, i].astype(jnp.float32).reshape(width, lanes).astype(jnp.bfloat16)
        return lax.dot_general(square[...], field, LAST, preferred_element_type=jnp.float32).astype(jnp.bfloat16)

    copies[0].wait()
    filter_one_grad[...] = whole(2)
    filter_two_grad[...] = whole(3)
    copies[1].wait()
    total = part_here[...]
    for i in (0, 1):
        copies[2 + i].wait()
        total += lax.dot_general(whole(i), w_in_here[i], LAST, preferred_element_type=jnp.float32)
    in_grad[...] = total.astype(jnp.bfloat16)


def place_kernel(taken, moves, w_in_grad):
    devices, group, lanes = taken.shape
    per, kinds = moves.shape[0], moves.shape[2] // lanes
    for g in range(devices // per):
        total = jnp.zeros((group, kinds * lanes), jnp.float32)
        for s in range(per):
            total += jnp.dot(taken[g * per + s], moves[s], preferred_element_type=jnp.float32)
        for f in range(kinds):
            at = f * devices * group + g * lanes
            w_in_grad[:, at : at + lanes] = total[:, f * lanes : (f + 1) * lanes]


def moves_of(group, lanes, kinds):
    per = lanes // group
    table = np.zeros((per, lanes, kinds * lanes), np.float32)
    for s in range(per):
        for f in range(kinds):
            for c in range(group):
                table[s, f * group + c, f * lanes + s * group + c] = 1.0
    return jnp.asarray(table, jnp.bfloat16)


def bits_of(count):
    return [1 << i for i in range(count.bit_length() - 1)]


def swap(block, axis, bit):
    return lax.ppermute(block, axis, [(i, i ^ bit) for i in range(lax.axis_size(axis))])


def after(x, *others):
    return lax.optimization_barrier((x, *others))[0]


def chips_of(block):
    blocks = [block] + [None] * (lax.axis_size("minor") // 2 - 1)
    for j in range(len(blocks) - 1, 0, -1):
        if j & (j - 1) == 0:
            blocks[j] = swap(block, "minor", 2 * j)
    return blocks


def far_chips(blocks, later):
    blocks, first = list(blocks), []
    for j in range(1, len(blocks)):
        low = j & -j
        if j != low:
            block = after(blocks[j ^ low], later)
            first.append(swap(block[:16], "minor", 2 * low))
            blocks[j] = jnp.concatenate([first[-1], swap(block[16:], "minor", 2 * low)])
    return blocks, first


def major_near(blocks):
    half = max(len(blocks) // 2, 1)
    lines = []
    for part in (blocks[:half], blocks[half:]):
        whole = jnp.concatenate(part)
        held = [whole] + [None] * (lax.axis_size("major") - 1)
        for j in range(1, len(held)):
            if j & (j - 1) == 0:
                held[j] = swap(whole, "major", j)
        lines.append(held)
    return lines


def gather_chips(lines, later):
    pieces = []
    for turn, line in enumerate(lines):
        held = [piece if piece is None else after(piece, later) for piece in line]
        for j in range(1, len(held)):
            bit = j & -j if turn else 1 << (j.bit_length() - 1)
            if j != bit:
                held[j] = swap(held[j ^ bit], "major", bit)
        pieces.append(held)
    return [piece for pair in zip(*pieces) for piece in pair]


def out_part(second_out, cots):
    width, rows_dev = second_out.shape
    majors, minors = lax.axis_size("major"), lax.axis_size("minor")
    mine = lax.axis_index("major")
    slabs = second_out.reshape(majors, width // majors, rows_dev)
    slab = [lax.dynamic_index_in_dim(slabs, mine ^ j, 0, keepdims=False) for j in range(majors)]
    slab = jnp.stack([swap(part, "major", j) if j else part for j, part in enumerate(slab)])
    total = jnp.einsum("mct,mtw->cw", slab, jnp.stack(cots), preferred_element_type=jnp.float32)
    total = total.reshape(minors // 2, 2, -1, total.shape[1])
    mine = lax.axis_index("minor") % 2
    part = lambda core: lax.dynamic_index_in_dim(total, core, 1, keepdims=False)
    return part(mine) + swap(part(1 - mine), "minor", 1)


def out_parts(total):
    mine = lax.axis_index("minor") // 2
    part = lambda chip: lax.dynamic_index_in_dim(total, chip, 0, keepdims=False)
    return [part(mine)] + [swap(part(mine ^ j).astype(jnp.bfloat16), "minor", 2 * j) for j in range(1, total.shape[0])]


def regroup(x):
    return lax.all_to_all(x, AXES, split_axis=0, concat_axis=0, tiled=True)


def shards(block_in, out_cot, w_in, w_out, conv_one, conv_two, filter_one, filter_two):
    rows_dev, width = block_in.shape
    devices, majors = lax.axis_size(AXES), lax.axis_size("major")
    group = width // devices
    scale = (rows_dev * devices) ** (-0.5)
    fft_scale = scale / (rows_dev * devices)
    field = lambda *dims: jax.ShapeDtypeStruct((devices, *dims, group, rows_dev), jnp.bfloat16)
    array = lambda *dims: jax.ShapeDtypeStruct(dims, jnp.bfloat16)

    near_in = chips_of(block_in)
    square = jnp.eye(rows_dev, dtype=jnp.bfloat16)
    sent, second_out, late = on_chip(
        begin_kernel,
        [field(7), array(width, rows_dev), array(rows_dev, width)],
        (square, conv_one, filter_two, filter_one, out_cot, conv_two, block_in, w_out, w_in),
        [
            pltpu.VMEM((6, rows_dev, width), jnp.bfloat16),
            pltpu.VMEM((width, width), jnp.bfloat16),
            pltpu.VMEM((3, width, width), jnp.bfloat16),
            pltpu.SemaphoreType.DMA((10,)),
        ],
        range(1, 9),
        60,
    )
    cots = [swap(out_cot, "major", j) if j else out_cot for j in range(majors)]
    sent = after(sent, *cots, *[block for block in near_in if block is not None])
    near_in, first = far_chips(near_in, late)
    sent = after(sent, *first)
    here = regroup(sent)
    total = out_part(after(second_out, sent), cots)
    late = lax.dot_general(late, w_in[:, 2 * width :], LAST, preferred_element_type=jnp.float32)
    lines = major_near([after(block, sent) for block in near_in])
    here = after(here, late, total, *[piece for line in lines for piece in line if piece is not None])

    spec = pltpu.VMEM((devices * group, 2 * rows_dev), jnp.float32)
    back, slab = on_chip(
        functools.partial(middle_kernel, fft_scale),
        [field(4), array(rows_dev, devices * rows_dev)],
        (lax.axis_index(AXES).astype(jnp.int32)[None], here, *tables(devices, rows_dev)),
        [
            pltpu.VMEM((devices * group, rows_dev), jnp.float32),
            spec,
            spec,
            spec,
            pltpu.VMEM((devices, 4, group, rows_dev), jnp.bfloat16),
            pltpu.SemaphoreType.DMA((4,)),
        ],
        far_out=(0,),
    )
    all_in = gather_chips(lines, here)
    parts = out_parts(after(total, *[piece for piece in lines[0] if piece is not None]))
    back, *parts = lax.optimization_barrier((back, *parts, *all_in))[: 1 + len(parts)]
    w_out_grad = sum(part.astype(jnp.float32) for part in parts) * scale
    home = regroup(back)
    all_in += [swap(after(piece, back), "minor", 1) for piece in all_in]

    rows = all_in[0].shape[0]
    slots = min(len(all_in), 16 * 2**20 // (2 * rows * width))
    part = on_chip(
        functools.partial(slab_kernel, scale),
        field(),
        (slab, *all_in),
        [pltpu.VMEM((slots, rows, width), jnp.bfloat16), pltpu.SemaphoreType.DMA((len(all_in),))],
        range(1, 1 + len(all_in)),
        60,
    )
    taken = regroup(after(part, home))
    in_grad, filter_one_grad, filter_two_grad = on_chip(
        home_kernel,
        [array(rows_dev, width)] * 3,
        (square, home, late, w_in),
        [
            pltpu.VMEM(home.shape, jnp.bfloat16),
            pltpu.VMEM((rows_dev, width), jnp.float32),
            pltpu.VMEM((2, width, width), jnp.bfloat16),
            pltpu.SemaphoreType.DMA((4,)),
        ],
        range(1, 4),
        60,
    )
    w_in_grad = on_chip(
        place_kernel, jax.ShapeDtypeStruct((group, 3 * width), jnp.float32), (taken, moves_of(group, rows_dev, 3))
    )
    return in_grad, w_in_grad, w_out_grad, filter_one_grad, filter_two_grad


def solution(mesh):
    tokens = P(AXES, None)
    return jax.shard_map(
        shards,
        mesh=mesh,
        in_specs=(tokens, tokens, P(), P(), tokens, tokens, tokens, tokens),
        out_specs=(tokens,) * 5,
        check_vma=False,
    )
```
